256 devices in a mesh: row: 32 (over x, z), col: 8 (over y, core).
Axes of the slice: x: 4, y: 4, z: 8, core: 2. Of those that a mesh axis runs over, the one named last changes fastest.
Arguments:
- front: float32 [6, 32, 64, 12, 8, 128], P(None, 'row', None, None, 'col'), as said below
Outputs:
- factored: float32 [6, 32, 64, 12, 8, 128], P(None, 'row', None, None, 'col')
Inputs may be any that keep to these rules, and one draw needn't show every extreme that they name: `front`: read as A, the matrix is symmetric and positive definite.
All inputs are finite; a program needn't handle non-finite values.
Results may differ from the reference program's by a relative error of at most 0.0001.
Values sent between devices are 32-bit elements; how exact they have to be, the bound alone decides.
No kernel may reach another device: no remote copies, remote signals or barrier semaphores. Data moves between devices by JAX's collectives and lax.ppermute only.
A program may use at most 64 MiB of HBM per device.

```python
import math
import jax
import jax.numpy as jnp
from jax import lax

N = 12288
RB = 64
CB = 128
PANELS = 2
SUB = 256
PANEL = 512
KR = 6
KC = 12
N_ROW = 32
N_COL = 8


def draw_front(key, part):
    key_noise = jax.random.fold_in(key, 11)
    key_diag = jax.random.fold_in(key, 23)
    key_scale = jax.random.fold_in(key, 37)
    key_common = jax.random.fold_in(key, 41)
    noise = jnp.clip(0.5 * jax.random.normal(key_noise, (N, N), jnp.float32), -1.0, 1.0)
    common = jax.random.uniform(key_common, (N,), jnp.float32, 1.0, 3.0)
    lowest = 0.5
    highest = 2.0
    upper = jnp.triu(noise, 1)
    symmetric = upper + upper.T + jnp.outer(common, common)
    diagonal = jax.random.uniform(key_diag, (N,), jnp.float32, 2.2, 4.0) * math.sqrt(N)
    symmetric = symmetric + jnp.diag(diagonal)
    scales = jnp.exp(jax.random.uniform(key_scale, (N,), jnp.float32, math.log(lowest), math.log(highest)))
    scaled = symmetric * scales[:, None] * scales[None, :]
    return scaled.reshape(KR, N_ROW, RB, KC, N_COL, CB)


def setup_inputs(seed: int = 0) -> dict:
    splits = jax.random.split(jax.random.key(seed), 2)
    front = draw_front(jax.random.fold_in(splits[1], 71), 0)
    return {"front": front}


def factor_block(block):
    lower_f = jnp.linalg.cholesky(block)
    inverse = jax.scipy.linalg.solve_triangular(lower_f, jnp.eye(block.shape[0], dtype=block.dtype), lower=True)
    return (lower_f, inverse)

def reference(front):
    highest = lax.Precision.HIGHEST
    matrix = front.reshape(N, N)
    for panel_index in range(PANELS):
        anchor = panel_index * PANEL
        factors = []
        for halfway in range(2):
            leading = anchor + halfway * SUB
            block_cols = matrix[:, leading:leading + SUB]
            if halfway == 1:
                block_cols = block_cols - jnp.dot(factors[0], factors[0][leading:leading + SUB].T, precision=highest)
            lower_f, inverse = factor_block(block_cols[leading:leading + SUB])
            below_rows = jnp.dot(block_cols[leading + SUB:], inverse.T, precision=highest)
            factors.append(jnp.concatenate([jnp.zeros((leading, SUB), matrix.dtype), lower_f, below_rows], axis=0))
        lpanel = jnp.concatenate(factors, axis=1)

        def update(operands):
            rows_blk, panel_rows = operands
            return rows_blk - jnp.dot(panel_rows, lpanel.T, precision=highest)
        matrix = lax.map(update, (matrix.reshape(N // PANEL, PANEL, N), lpanel.reshape(N // PANEL, PANEL, PANEL))).reshape(N, N)
        matrix = matrix.at[:, anchor:anchor + PANEL].set(lpanel)
    finished = PANELS * PANEL
    indices = jnp.arange(N)
    retain = (indices[:, None] >= finished) | (indices[None, :] < finished)
    matrix = jnp.where(retain, matrix, jnp.zeros((), matrix.dtype))
    return matrix.reshape(front.shape)
```

```python
import functools

import jax
import jax.numpy as jnp
from jax import lax
from jax.experimental import pallas as pl
from jax.experimental.pallas import tpu as pltpu
from jax.sharding import PartitionSpec as P

B = 128
HALF = 512
FULL = 1024
F32 = jnp.float32
BF16 = jnp.bfloat16
VMEM = pl.BlockSpec(memory_space=pltpu.VMEM)
SMEM = pl.BlockSpec(memory_space=pltpu.SMEM)
LIMIT = 56 * 1024 * 1024


def lane(tile, c):
    return jnp.broadcast_to(tile[:, c : c + 1], (8, B))


def sub(tile, i):
    return jnp.broadcast_to(tile[i : i + 1, :], (8, B))


def exact(left, right, dims):
    return lax.dot_general(
        left, right, (dims, ((), ())), precision=lax.Precision.HIGHEST, preferred_element_type=F32
    )


def split(value):
    high = value.astype(BF16)
    return high, (value - high.astype(F32)).astype(BF16)


def dot3(left, right, dims):
    mul = lambda a, b: lax.dot_general(a, b, (dims, ((), ())), preferred_element_type=F32)
    return mul(left[0], right[0]) + (mul(left[0], right[1]) + mul(left[1], right[0]))


def factor_block(rows):
    rows = list(rows)
    col = lax.broadcasted_iota(jnp.int32, (8, B), 1)
    row = lax.broadcasted_iota(jnp.int32, (8, B), 0)
    uppers, inverses = [], []
    for p in range(16):
        top = rows[p]
        o = 8 * p
        inside = (col >= o) & (col < o + 8)
        cols = [lane(top, o + j) for j in range(8)]
        a = {(i, j): sub(cols[j], i) for j in range(8) for i in range(j, 8)}
        unit = jnp.where(inside, (col - o == row).astype(F32), top)
        m, inv = {}, []
        for j in range(8):
            rcp = 1.0 / a[j, j]
            inv.append(rcp)
            for i in range(j + 1, 8):
                m[i, j] = a[i, j] * rcp
            for k in range(j + 1, 8):
                for i in range(k, 8):
                    a[i, k] = a[i, k] - m[i, j] * a[k, j]
        n = {}
        for j in range(8):
            for i in range(j + 1, 8):
                acc = m[i, j]
                for k in range(j + 1, i):
                    acc = acc + m[i, k] * n[k, j]
                n[i, j] = -acc
        spread = [sub(unit, j) for j in range(8)]
        z = []
        for i in range(8):
            acc = spread[i]
            for k in range(i):
                acc = acc + n[i, k] * spread[k]
            z.append(acc)
        scaled = [z[i] * inv[i] for i in range(8)]
        v = []
        for j in range(8):
            acc = scaled[j]
            for i in range(j + 1, 8):
                acc = acc + n[i, j] * scaled[i]
            v.append(acc)
        for q in range(p + 1, 16):
            t = [lane(rows[q], o + j) * v[j] for j in range(8)]
            s = ((t[0] + t[1]) + (t[2] + t[3])) + ((t[4] + t[5]) + (t[6] + t[7]))
            rows[q] = jnp.where(inside, 0.0, rows[q]) - s
        roots = [lax.rsqrt(a[j, j]) for j in range(8)]
        w = z[0] * roots[0]
        for i in range(1, 8):
            w = jnp.where(row == i, z[i] * roots[i], w)
        u = w
        for i in range(8):
            root = a[i, i] * roots[i]
            u = jnp.where((row == i) & (col == o + i), root, u)
            for j in range(i + 1, 8):
                u = jnp.where((row == i) & (col == o + j), root * m[j, i], u)
        uppers.append(jnp.where(col >= o + row, u, 0.0))
        inverses.append(jnp.where(col <= o + row, w, 0.0))
    return uppers, inverses


def factor_half(s_ref, u_ref, w_ref):
    blocks = HALF // B

    @pl.loop(0, blocks)
    def _(k):
        o = pl.multiple_of(k * B, B)
        here = pl.ds(o, B)
        tiles = [s_ref[pl.ds(pl.multiple_of(o + 8 * i, 8), 8), here] for i in range(16)]
        uppers, inverses = factor_block(tiles)
        u_diag = jnp.concatenate(uppers, axis=0)
        w_diag = jnp.concatenate(inverses, axis=0)
        s_ref[here, here] = jnp.eye(B, dtype=F32)
        made = exact(w_diag, s_ref[here, :], ((1,), (0,)))
        s_ref[here, :] = made
        block = lax.broadcasted_iota(jnp.int32, (B, HALF), 1) // B
        u_ref[here, :] = jnp.where(block > k, made, 0.0)
        w_ref[here, :] = jnp.where(block <= k, made, 0.0)
        u_ref[here, here] = u_diag

        @pl.loop(k + 1, blocks)
        def _(i):
            there = pl.ds(pl.multiple_of(i * B, B), B)
            mult = s_ref[here, there]
            s_ref[there, here] = jnp.zeros((B, B), F32)
            s_ref[there, :] = s_ref[there, :] - exact(mult, made, ((0,), (0,)))


def place(where_ref, own_ref, other_ref, dst_ref, count):
    z4 = where_ref[1] & 3
    core = where_ref[3]
    for s in range(4):
        for h in range(2):
            for y in range(count):
                r = pl.ds(pl.multiple_of(h * 256 + (z4 ^ s) * 64, 64), 64)
                dst_ref[r, pl.ds(pl.multiple_of(y * 256 + core * B, B), B)] = own_ref[s, h, y]
                dst_ref[r, pl.ds(pl.multiple_of(y * 256 + (1 - core) * B, B), B)] = other_ref[s, h, y]


def first_kernel(where_ref, own_ref, other_ref, u_ref, w_ref, s_ref):
    place(where_ref, own_ref, other_ref, s_ref, 2)
    factor_half(s_ref, u_ref, w_ref)


def first_half(where, own, other):
    shape = jax.ShapeDtypeStruct((HALF, HALF), F32)
    return pl.pallas_call(
        first_kernel,
        out_shape=(shape, shape),
        in_specs=[SMEM, VMEM, VMEM],
        out_specs=(VMEM, VMEM),
        scratch_shapes=[pltpu.VMEM((HALF, HALF), F32)],
        compiler_params=pltpu.CompilerParams(vmem_limit_bytes=LIMIT),
        name="first_half",
    )(where, own, other)


def second_kernel(where_ref, own_ref, other_ref, ua_ref, wa_ref, u_ref, w_ref, raw_ref, s_ref, ub_ref, wb_ref):
    place(where_ref, own_ref, other_ref, raw_ref, 4)
    cross = exact(wa_ref[...], raw_ref[:, :HALF], ((1,), (1,)))
    u_ref[:HALF, HALF:] = cross
    s_ref[...] = raw_ref[:, HALF:] - exact(cross, cross, ((0,), (0,)))
    factor_half(s_ref, ub_ref, wb_ref)
    u_ref[:HALF, :HALF] = ua_ref[...]
    u_ref[HALF:, :HALF] = jnp.zeros((HALF, HALF), F32)
    u_ref[HALF:, HALF:] = ub_ref[...]
    w_ref[:HALF, :HALF] = wa_ref[...]
    w_ref[:HALF, HALF:] = jnp.zeros((HALF, HALF), F32)
    w_ref[HALF:, HALF:] = wb_ref[...]
    part = exact(u_ref[:HALF, HALF:], wa_ref[...], ((0,), (0,)))
    w_ref[HALF:, :HALF] = -exact(wb_ref[...], part, ((1,), (0,)))


def second_half(where, own, other, ua, wa):
    shape = jax.ShapeDtypeStruct((FULL, FULL), F32)
    half = pltpu.VMEM((HALF, HALF), F32)
    return pl.pallas_call(
        second_kernel,
        out_shape=(shape, shape),
        in_specs=[SMEM] + [VMEM] * 4,
        out_specs=(VMEM, VMEM),
        scratch_shapes=[pltpu.VMEM((HALF, FULL), F32), half, half, half],
        compiler_params=pltpu.CompilerParams(vmem_limit_bytes=LIMIT),
        name="second_half",
    )(where, own, other, ua, wa)


def rows_kernel(where_ref, own_ref, other_ref, u_ref, w_ref, high_ref, low_ref, slab_ref, a_ref, x_ref):
    y = where_ref[2]
    core = where_ref[3]
    for s in range(4):
        base = ((y - s) & 3) * 256
        a_ref[:, pl.ds(pl.multiple_of(base + core * B, B), B)] = own_ref[s]
        a_ref[:, pl.ds(pl.multiple_of(base + (1 - core) * B, B), B)] = other_ref[s]
    step = 256
    for k in range(0, FULL, step):
        x_ref[:, k : k + step] = dot3(
            split(a_ref[:, : k + step]), split(w_ref[k : k + step, : k + step]), ((1,), (1,))
        )
    for j in range(0, FULL, step):
        value = dot3(split(x_ref[:, j:]), split(w_ref[j:, j : j + step]), ((1,), (0,)))
        high, low = split(value)
        high_ref[:, j : j + step] = high
        low_ref[:, j : j + step] = low
    row_rank = where_ref[0] * 8 + where_ref[1]
    mine = pl.ds(pl.multiple_of((y * 2 + core) * B, B), B)
    slab_ref[...] = x_ref[:, mine]

    @pl.when(row_rank < 16)
    def _():
        block = u_ref[mine, pl.ds(pl.multiple_of((row_rank // 2) * B, B), B)].T
        slab_ref[:64, :] = jnp.where(row_rank % 2 == 0, block[:64], block[64:])


def row_factor(where, own, other, u, w):
    rows = own.shape[1]
    return pl.pallas_call(
        rows_kernel,
        out_shape=(
            jax.ShapeDtypeStruct((rows, FULL), BF16),
            jax.ShapeDtypeStruct((rows, FULL), BF16),
            jax.ShapeDtypeStruct((rows, B), F32),
        ),
        in_specs=[SMEM] + [VMEM] * 4,
        out_specs=(VMEM, VMEM, VMEM),
        scratch_shapes=[pltpu.VMEM((rows, FULL), F32), pltpu.VMEM((rows, FULL), F32)],
        compiler_params=pltpu.CompilerParams(vmem_limit_bytes=LIMIT),
        name="row_factor",
    )(where, own, other, u, w)


def trailing_kernel(where_ref, a_ref, bulk_ref, high_ref, low_ref, slab_ref, out_ref, bh_ref, bl_ref):
    rows = high_ref.shape[0]
    blocks = a_ref.shape[0] // rows
    row_rank = where_ref[0] * 8 + where_ref[1]
    gone = (row_rank < 16) & (lax.broadcasted_iota(jnp.int32, (rows, B), 0) < 64)

    def load(d, at):
        for p in range(2):
            for z in range(8):
                for part in range(2):
                    if part == 0:
                        source = 8 * p + z
                    else:
                        source = (24 if p == 0 else 16) + z
                    piece = bulk_ref[source, pl.ds(d, 32, stride=blocks), :]
                    high, low = split(piece)
                    r = HALF * p + 64 * z + 32 * part
                    bh_ref[r : r + 32, at : at + B] = high
                    bl_ref[r : r + 32, at : at + B] = low

    @pl.loop(0, blocks // 2)
    def _(pair):
        load(2 * pair, 0)
        load(2 * pair + 1, B)
        made = dot3((high_ref[...], low_ref[...]), (bh_ref[...], bl_ref[...]), ((1,), (0,)))
        for t in range(2):
            at = pl.ds(2 * pair + t, rows, stride=blocks)
            value = a_ref[at, :] - made[:, t * B : (t + 1) * B]
            out_ref[at, :] = jnp.where(gone, 0.0, value)

    out_ref[pl.ds(0, rows, stride=blocks), :] = slab_ref[...]


def trailing(where, a, bulk, high, low, slab):
    return pl.pallas_call(
        trailing_kernel,
        out_shape=jax.ShapeDtypeStruct(a.shape, F32),
        in_specs=[SMEM] + [VMEM] * 5,
        out_specs=VMEM,
        scratch_shapes=[pltpu.VMEM((FULL, 2 * B), BF16), pltpu.VMEM((FULL, 2 * B), BF16)],
        compiler_params=pltpu.CompilerParams(vmem_limit_bytes=LIMIT),
        name="trailing",
    )(where, a, bulk, high, low, slab)


def row_pairs(f):
    return [(x * 8 + z, (f(x, z)[0] % 4) * 8 + f(x, z)[1] % 8) for x in range(4) for z in range(8)]


def col_shift(s):
    return [(c, (c + 2 * s) % 8) for c in range(8)]


def swap_core(value):
    return lax.ppermute(value, "col", [(c, c ^ 1) for c in range(8)])


def from_x(source, target):
    return [(source * 8 + z, target * 8 + z) for z in range(8)]


def shards(front):
    lin = front.reshape(-1, B)
    rows = 384
    r = lax.axis_index("row")
    c = lax.axis_index("col")
    x, z, y, core = r // 8, r % 8, c // 2, c % 2
    where = jnp.stack([x, z, y, core]).astype(jnp.int32)

    slab = lax.slice(lin, (0, 0), lin.shape, (lin.shape[0] // rows, 1))
    piece = slab[:64]
    near = [piece] + [lax.ppermute(piece, "col", col_shift(s)) for s in (3, 2, 1)]
    ring = jnp.stack(near + near[:3])
    mine = lax.dynamic_slice_in_dim(ring, (4 - y) % 4, 4, 0)

    top = lin[:768]
    moved = lax.ppermute(top[384:], "row", from_x(0, 3) + from_x(1, 2))
    bulk = lax.all_gather(jnp.where(x >= 2, moved, top[:384]), "row", axis=0)

    across = lax.ppermute(mine, "row", row_pairs(lambda x, z: (x, z + 4)))
    both = jnp.where(z < 4, jnp.stack([mine, across]), jnp.stack([across, mine]))

    def broadcast_x(value, source):
        got = [lax.ppermute(value, "row", from_x(source, t)) for t in range(4) if t != source]
        out = value
        for t, g in zip([t for t in range(4) if t != source], got):
            out = jnp.where(x == t, g, out)
        return out

    def gather_z4(value):
        return jnp.stack(
            [value] + [lax.ppermute(value, "row", row_pairs(lambda x, z: (x, z ^ s))) for s in (1, 2, 3)]
        )

    part_a = gather_z4(broadcast_x(both[:, :2], 0))
    part_b = gather_z4(broadcast_x(both, 1))
    ua, wa = first_half(where, part_a, swap_core(part_a))
    u, w = second_half(where, part_b, swap_core(part_b), ua, wa)

    wide = jnp.stack([slab] + [lax.ppermute(slab, "col", col_shift(s)) for s in (1, 2, 3)])
    high, low, own_slab = row_factor(where, wide, swap_core(wide), u, w)
    out = trailing(where, lin, bulk, high, low, own_slab)
    return out.reshape(front.shape)


def solution(mesh):
    spec = P(None, "row", None, None, "col", None)
    return jax.shard_map(shards, mesh=mesh, in_specs=(spec,), out_specs=spec, check_vma=False)
```

```python
import functools

import jax
import jax.numpy as jnp
from jax import lax
from jax.experimental import pallas as pl
from jax.experimental.pallas import tpu as pltpu
from jax.sharding import PartitionSpec as P

B = 128
HALF = 512
FULL = 1024
F32 = jnp.float32
BF16 = jnp.bfloat16
VMEM = pl.BlockSpec(memory_space=pltpu.VMEM)
SMEM = pl.BlockSpec(memory_space=pltpu.SMEM)
LIMIT = 56 * 1024 * 1024


def lane(tile, c):
    return jnp.broadcast_to(tile[:, c : c + 1], (8, B))


def sub(tile, i):
    return jnp.broadcast_to(tile[i : i + 1, :], (8, B))


def exact(left, right, dims):
    return lax.dot_general(
        left, right, (dims, ((), ())), precision=lax.Precision.HIGHEST, preferred_element_type=F32
    )


def split(value):
    high = value.astype(BF16)
    return high, (value - high.astype(F32)).astype(BF16)


def dot3(left, right, dims):
    mul = lambda a, b: lax.dot_general(a, b, (dims, ((), ())), preferred_element_type=F32)
    return mul(left[0], right[0]) + (mul(left[0], right[1]) + mul(left[1], right[0]))


def factor_block(rows, one):
    rows = list(rows)
    col = lax.broadcasted_iota(jnp.int32, (8, B), 1)
    row = lax.broadcasted_iota(jnp.int32, (8, B), 0)
    uppers, inverses = [], []
    for p in range(16):
        top = rows[p]
        o = 8 * p
        inside = (col >= o) & (col < o + 8)
        cols = [lane(top, o + j) * one for j in range(8)]
        a = {(i, j): sub(cols[j], i) for j in range(8) for i in range(j, 8)}
        unit = jnp.where(inside, (col - o == row).astype(F32), top)
        z = [sub(unit, j) for j in range(8)]
        more = p + 1 < 16
        if more:
            c = [lane(rows[p + 1], o + j) for j in range(8)]
            below = jnp.where(inside, 0.0, rows[p + 1])
        m, inv = {}, []
        for j in range(8):
            rcp = 1.0 / a[j, j]
            inv.append(rcp)
            for i in range(j + 1, 8):
                m[i, j] = a[i, j] * rcp
            if more:
                below = below - (c[j] * rcp) * z[j]
            for i in range(j + 1, 8):
                for k in range(j + 1, i + 1):
                    a[i, k] = a[i, k] - m[i, j] * a[k, j]
            for i in range(j + 1, 8):
                z[i] = z[i] - m[i, j] * z[j]
                if more:
                    c[i] = c[i] - m[i, j] * c[j]
        if more:
            rows[p + 1] = below
        if p + 2 < 16:
            v = [None] * 8
            for j in range(7, -1, -1):
                acc = z[j] * inv[j]
                for i in range(7, j, -1):
                    acc = acc - m[i, j] * v[i]
                v[j] = acc
            for q in range(p + 2, 16):
                t = [lane(rows[q], o + j) * v[j] for j in range(8)]
                s = ((t[0] + t[1]) + (t[2] + t[3])) + ((t[4] + t[5]) + (t[6] + t[7]))
                rows[q] = jnp.where(inside, 0.0, rows[q]) - s
        roots = [lax.rsqrt(a[j, j]) for j in range(8)]
        w = z[0] * roots[0]
        for i in range(1, 8):
            w = jnp.where(row == i, z[i] * roots[i], w)
        scale = a[0, 0] * roots[0]
        for i in range(1, 8):
            scale = jnp.where(row == i, a[i, i] * roots[i], scale)
        u = w
        for j in range(8):
            entries = jnp.ones((8, B), F32)
            for i in range(j):
                entries = jnp.where(row == i, m[j, i], entries)
            u = jnp.where(col == o + j, entries * scale, u)
        uppers.append(jnp.where(col >= o + row, u, 0.0))
        inverses.append(jnp.where(col <= o + row, w, 0.0))
    return jnp.concatenate(uppers, axis=0), jnp.concatenate(inverses, axis=0)


def factor_half(where_ref, s_ref, u_ref, w_ref):
    one = jnp.full((8, B), 1.0, F32) * jnp.where(where_ref[0] >= 0, 1.0, 0.0)
    count = HALF // B
    at = lambda i: slice(i * B, (i + 1) * B)
    for k in range(count):
        here = at(k)
        upper, inverse = factor_block([s_ref[k * B + 8 * i : k * B + 8 * i + 8, here] for i in range(16)], one)
        u_ref[here, here] = upper
        w_ref[here, here] = inverse
        if k:
            u_ref[here, : k * B] = jnp.zeros((B, k * B), F32)
            w_ref[here, : k * B] = exact(inverse, s_ref[here, : k * B], ((1,), (0,)))
        if k + 1 == count:
            break
        e = (k + 1) * B
        w_ref[here, e:] = jnp.zeros((B, HALF - e), F32)
        follow = exact(inverse, s_ref[here, at(k + 1)], ((1,), (0,)))
        u_ref[here, at(k + 1)] = follow
        s_ref[at(k + 1), at(k + 1)] = s_ref[at(k + 1), at(k + 1)] - exact(follow, follow, ((0,), (0,)))
        if e + B < HALF:
            u_ref[here, e + B :] = exact(inverse, s_ref[here, e + B :], ((1,), (0,)))
        for i in range(k + 1, count):
            mult = u_ref[here, at(i)]
            begin = max(i, k + 2) * B
            if begin < HALF:
                s_ref[at(i), begin:] = s_ref[at(i), begin:] - exact(mult, u_ref[here, begin:], ((0,), (0,)))
            if k:
                s_ref[at(i), : k * B] = s_ref[at(i), : k * B] - exact(mult, w_ref[here, : k * B], ((0,), (0,)))
            s_ref[at(i), here] = -exact(mult, inverse, ((0,), (0,)))


def call(kernel, name, outs, scratch, *args):
    shapes = tuple(jax.ShapeDtypeStruct(shape, dtype) for shape, dtype in outs)
    return pl.pallas_call(
        kernel,
        out_shape=shapes,
        in_specs=[SMEM] + [VMEM] * (len(args) - 1),
        out_specs=tuple(VMEM for _ in outs),
        scratch_shapes=[pltpu.VMEM(shape, dtype) for shape, dtype in scratch],
        compiler_params=pltpu.CompilerParams(vmem_limit_bytes=LIMIT),
        name=name,
    )(*args)


def prepare_kernel(where_ref, top_ref, moved_ref, g1_ref, g2_ref, g3_ref, mine_ref, share_ref):
    z4 = where_ref[1] & 3
    for s, ref in enumerate((None, g1_ref, g2_ref, g3_ref)):
        piece = top_ref[pl.ds(0, 64, stride=12), :] if ref is None else ref[...]
        mine_ref[pl.ds(z4 ^ s, 1)] = piece[None]
    for d in range(12):
        share_ref[d] = jnp.where(
            where_ref[0] >= 2, moved_ref[pl.ds(d, 32, stride=12), :], top_ref[pl.ds(d, 32, stride=12), :]
        )


def choose_kernel(where_ref, own_ref, plus_ref, minus_ref, two_ref, a_ref, b_ref):
    orders = (
        (own_ref, minus_ref),
        (plus_ref, own_ref),
        (two_ref, plus_ref),
        (minus_ref, two_ref),
    )
    for x, (first, second) in enumerate(orders):

        @pl.when(where_ref[0] == x)
        def _():
            a_ref[...] = first[...]
            b_ref[...] = second[...]


def pack_kernel(
    where_ref, a_ref, g1_ref, g2_ref, g3_ref, b_ref, bo_ref, slab_ref, so_ref, a2_ref, b2_ref, s2_ref
):
    y = where_ref[2]
    core = where_ref[3]
    for s, ref in enumerate((a_ref, g1_ref, g2_ref, g3_ref)):
        for target in range(2):

            @pl.when(((y - target) & 3) == s)
            def _():
                a2_ref[target] = ref[...]

    for own, other, out in ((b_ref, bo_ref, b2_ref), (slab_ref, so_ref, s2_ref)):
        out[pl.ds(core, 1)] = own[...][None]
        out[pl.ds(1 - core, 1)] = other[...][None]


def first_kernel(where_ref, own_ref, other_ref, rows_ref, u_ref, w_ref, again_ref, s_ref):
    core = where_ref[3]
    for y in range(2):
        s_ref[:, pl.ds(pl.multiple_of(y * 256 + core * B, B), B)] = own_ref[y]
        s_ref[:, pl.ds(pl.multiple_of(y * 256 + (1 - core) * B, B), B)] = other_ref[y]
    again_ref[...] = rows_ref[...]
    factor_half(where_ref, s_ref, u_ref, w_ref)


def second_kernel(
    where_ref, g0_ref, g1_ref, g2_ref, g3_ref, ua_ref, wa_ref, u_ref, w_ref, raw_ref, s_ref, ub_ref, wb_ref
):
    for s, ref in enumerate((g0_ref, g1_ref, g2_ref, g3_ref)):
        for core in range(2):
            lanes = pl.ds(pl.multiple_of(((where_ref[2] - s) & 3) * 256 + core * B, B), B)
            raw_ref[:, lanes] = ref[core]
    cross = exact(wa_ref[...], raw_ref[:, :HALF], ((1,), (1,)))
    u_ref[:HALF, HALF:] = cross
    s_ref[...] = raw_ref[:, HALF:] - exact(cross, cross, ((0,), (0,)))
    part = dot3(split(cross), split(wa_ref[...]), ((0,), (0,)))
    factor_half(where_ref, s_ref, ub_ref, wb_ref)
    u_ref[:HALF, :HALF] = ua_ref[...]
    u_ref[HALF:, :HALF] = jnp.zeros((HALF, HALF), F32)
    u_ref[HALF:, HALF:] = ub_ref[...]
    w_ref[:HALF, :HALF] = wa_ref[...]
    w_ref[:HALF, HALF:] = jnp.zeros((HALF, HALF), F32)
    w_ref[HALF:, HALF:] = wb_ref[...]
    w_ref[HALF:, :HALF] = -dot3(split(wb_ref[...]), split(part), ((1,), (0,)))


def rows_kernel(
    where_ref, g0_ref, g1_ref, g2_ref, g3_ref, u_ref, w_ref,
    high_ref, low_ref, slab_ref, ah_ref, al_ref, wh_ref, wl_ref, x_ref,
):
    y = where_ref[2]
    core = where_ref[3]
    for s, ref in enumerate((g0_ref, g1_ref, g2_ref, g3_ref)):
        for at in range(2):
            lanes = pl.ds(pl.multiple_of(((y - s) & 3) * 256 + at * B, B), B)
            ah_ref[:, lanes], al_ref[:, lanes] = split(ref[at])
    step = 256
    for k in range(0, FULL, step):
        wh_ref[k : k + step, :], wl_ref[k : k + step, :] = split(w_ref[k : k + step, :])
    for k in range(0, FULL, step):
        e = k + step
        x_ref[:, k:e] = dot3((ah_ref[:, :e], al_ref[:, :e]), (wh_ref[k:e, :e], wl_ref[k:e, :e]), ((1,), (1,)))
    row_rank = where_ref[0] * 8 + where_ref[1]
    mine = pl.ds(pl.multiple_of((y * 2 + core) * B, B), B)
    slab_ref[...] = x_ref[:, mine]
    for k in range(0, FULL, step):
        e = k + step
        ah_ref[:, k:e], al_ref[:, k:e] = split(x_ref[:, k:e])
    for j in range(0, FULL, step):
        e = j + step
        value = dot3((ah_ref[:, j:], al_ref[:, j:]), (wh_ref[j:, j:e], wl_ref[j:, j:e]), ((1,), (0,)))
        high_ref[:, j:e], low_ref[:, j:e] = split(value)

    @pl.when(row_rank < 16)
    def _():
        block = u_ref[mine, pl.ds(pl.multiple_of((row_rank // 2) * B, B), B)].T
        slab_ref[:64, :] = jnp.where(row_rank % 2 == 0, block[:64], block[64:])


def trailing_kernel(where_ref, a_ref, bulk_ref, high_ref, low_ref, slab_ref, out_ref, bh_ref, bl_ref):
    rows = high_ref.shape[0]
    row_rank = where_ref[0] * 8 + where_ref[1]
    gone = (row_rank < 16) & (lax.broadcasted_iota(jnp.int32, (rows, B), 0) < 64)
    pair = pl.program_id(0)
    for p in range(2):
        for z in range(8):
            for part in range(2):
                source = (8 * p if part == 0 else 24 - 8 * p) + z
                r = HALF * p + 64 * z + 32 * part
                for t in range(2):
                    high, low = split(bulk_ref[source, t])
                    bh_ref[r : r + 32, t * B : (t + 1) * B] = high
                    bl_ref[r : r + 32, t * B : (t + 1) * B] = low
    made = dot3((high_ref[...], low_ref[...]), (bh_ref[...], bl_ref[...]), ((1,), (0,)))
    for t in range(2):
        at = pl.ds(2 * pair + t, rows, stride=12)
        value = a_ref[at, :] - made[:, t * B : (t + 1) * B]
        out_ref[at, :] = jnp.where(gone, 0.0, value)

    @pl.when(pair == 0)
    def _():
        out_ref[pl.ds(0, rows, stride=12), :] = slab_ref[...]


def trailing(where, a, bulk, high, low, slab):
    whole = lambda v: pl.BlockSpec(v.shape, lambda i: (0,) * v.ndim)
    return pl.pallas_call(
        trailing_kernel,
        out_shape=jax.ShapeDtypeStruct(a.shape, F32),
        grid=(6,),
        in_specs=[
            SMEM,
            whole(a),
            pl.BlockSpec((32, 2, 32, B), lambda i: (0, i, 0, 0)),
            whole(high),
            whole(low),
            whole(slab),
        ],
        out_specs=whole(a),
        scratch_shapes=[pltpu.VMEM((FULL, 2 * B), BF16), pltpu.VMEM((FULL, 2 * B), BF16)],
        compiler_params=pltpu.CompilerParams(vmem_limit_bytes=LIMIT),
        name="trailing",
    )(where, a, bulk, high, low, slab)


def row_pairs(f):
    return [(x * 8 + z, (f(x, z)[0] % 4) * 8 + f(x, z)[1] % 8) for x in range(4) for z in range(8)]


def col_shift(s):
    return [(c, (c + 2 * s) % 8) for c in range(8)]


def swap_core(value):
    return lax.ppermute(value, "col", [(c, c ^ 1) for c in range(8)])


def from_x(source, target):
    return [(source * 8 + z, target * 8 + z) for z in range(8)]


def shards(front):
    lin = front.reshape(-1, B)
    rows = 384
    r = lax.axis_index("row")
    c = lax.axis_index("col")
    x, z, y, core = r // 8, r % 8, c // 2, c % 2
    where = jnp.stack([x, z, y, core]).astype(jnp.int32)

    top = lin[:768]
    piece = lax.slice(lin, (0, 0), (768, B), (12, 1))
    near = [lax.ppermute(piece, "row", row_pairs(lambda x, z: (x, z ^ s))) for s in (1, 2, 3)]
    moved = lax.ppermute(top[384:], "row", from_x(0, 3) + from_x(1, 2))
    mine, share = call(
        prepare_kernel, "prepare", [((4, 64, B), F32), ((12, 32, B), F32)], [], where, top, moved, *near
    )
    bulk = lax.all_gather(share, "row", axis=0)

    across = lax.ppermute(mine, "row", row_pairs(lambda x, z: (x, z + 4)))
    both = jnp.where(z < 4, jnp.stack([mine, across]), jnp.stack([across, mine])).reshape(HALF, B)
    got = [lax.ppermute(both, "row", row_pairs(lambda x, z: (x + s, z))) for s in (1, 3, 2)]
    block = ((HALF, B), F32)
    a, b = call(choose_kernel, "choose", [block, block], [], where, both, *got)
    slab = lax.slice(lin, (0, 0), lin.shape, (12, 1))
    near = [
        lax.ppermute(a, "col", [(c, (c + 2 * s) % 8) for c in range(4)]) for s in (1, 2, 3)
    ]
    pair = ((2, HALF, B), F32)
    a2, b2, s2 = call(
        pack_kernel, "pack", [pair, pair, ((2, rows, B), F32)], [],
        where, a, *near, b, swap_core(b), slab, swap_core(slab),
    )
    near_b = [lax.ppermute(b2, "col", col_shift(s)) for s in (1, 2, 3)]
    square = ((HALF, HALF), F32)
    ua, wa, s2 = call(
        first_kernel, "first", [square, square, (s2.shape, F32)], [square], where, a2, swap_core(a2), s2
    )
    near_s = [lax.ppermute(s2, "col", col_shift(s)) for s in (1, 2, 3)]
    whole = ((FULL, FULL), F32)
    u, w = call(
        second_kernel, "second", [whole] * 2, [((HALF, FULL), F32), square, square, square],
        where, b2, *near_b, ua, wa,
    )
    high, low, own_slab = call(
        rows_kernel, "rows", [((rows, FULL), BF16), ((rows, FULL), BF16), ((rows, B), F32)],
        [((rows, FULL), BF16)] * 2 + [((FULL, FULL), BF16)] * 2 + [((rows, FULL), F32)],
        where, s2, *near_s, u, w,
    )
    out = trailing(where, lin, bulk, high, low, own_slab)
    return out.reshape(front.shape)


def solution(mesh):
    spec = P(None, "row", None, None, "col", None)
    return jax.shard_map(shards, mesh=mesh, in_specs=(spec,), out_specs=spec, check_vma=False)
```

```python
import functools

import jax
import jax.numpy as jnp
from jax import lax
from jax.experimental import pallas as pl
from jax.experimental.pallas import tpu as pltpu
from jax.sharding import PartitionSpec as P

B = 128
HALF = 512
FULL = 1024
F32 = jnp.float32
BF16 = jnp.bfloat16
VMEM = pl.BlockSpec(memory_space=pltpu.VMEM)
SMEM = pl.BlockSpec(memory_space=pltpu.SMEM)
LIMIT = 30 * 1024 * 1024


def lane(tile, c):
    return jnp.broadcast_to(tile[:, c : c + 1], (8, B))


def sub(tile, i):
    return jnp.broadcast_to(tile[i : i + 1, :], (8, B))


def exact(left, right, dims):
    return lax.dot_general(
        left, right, (dims, ((), ())), precision=lax.Precision.HIGHEST, preferred_element_type=F32
    )


def split(value):
    high = value.astype(BF16)
    return high, (value - high.astype(F32)).astype(BF16)


def dot3(left, right, dims):
    mul = lambda a, b: lax.dot_general(a, b, (dims, ((), ())), preferred_element_type=F32)
    return mul(left[0], right[0]) + (mul(left[0], right[1]) + mul(left[1], right[0]))


def factor_block(rows, one):
    rows = list(rows)
    col = lax.broadcasted_iota(jnp.int32, (8, B), 1)
    row = lax.broadcasted_iota(jnp.int32, (8, B), 0)
    uppers, inverses = [], []
    for p in range(16):
        top = rows[p]
        o = 8 * p
        inside = (col >= o) & (col < o + 8)
        cols = [lane(top, o + j) * one for j in range(8)]
        a = {(i, j): sub(cols[j], i) for j in range(8) for i in range(j, 8)}
        unit = jnp.where(inside, (col - o == row).astype(F32), top)
        z = [sub(unit, j) for j in range(8)]
        more = p + 1 < 16
        if more:
            c = [lane(rows[p + 1], o + j) for j in range(8)]
            below = jnp.where(inside, 0.0, rows[p + 1])
        m, inv = {}, []
        for j in range(8):
            rcp = 1.0 / a[j, j]
            inv.append(rcp)
            for i in range(j + 1, 8):
                m[i, j] = a[i, j] * rcp
            if more:
                below = below - (c[j] * rcp) * z[j]
            for i in range(j + 1, 8):
                for k in range(j + 1, i + 1):
                    a[i, k] = a[i, k] - m[i, j] * a[k, j]
            for i in range(j + 1, 8):
                z[i] = z[i] - m[i, j] * z[j]
                if more:
                    c[i] = c[i] - m[i, j] * c[j]
        if more:
            rows[p + 1] = below
        if p + 2 < 16:
            v = [None] * 8
            for j in range(7, -1, -1):
                acc = z[j] * inv[j]
                for i in range(7, j, -1):
                    acc = acc - m[i, j] * v[i]
                v[j] = acc
            for q in range(p + 2, 16):
                t = [lane(rows[q], o + j) * v[j] for j in range(8)]
                s = ((t[0] + t[1]) + (t[2] + t[3])) + ((t[4] + t[5]) + (t[6] + t[7]))
                rows[q] = jnp.where(inside, 0.0, rows[q]) - s
        roots = [lax.rsqrt(a[j, j]) for j in range(8)]
        w = z[0] * roots[0]
        for i in range(1, 8):
            w = jnp.where(row == i, z[i] * roots[i], w)
        scale = a[0, 0] * roots[0]
        for i in range(1, 8):
            scale = jnp.where(row == i, a[i, i] * roots[i], scale)
        u = w
        for j in range(8):
            entries = jnp.ones((8, B), F32)
            for i in range(j):
                entries = jnp.where(row == i, m[j, i], entries)
            u = jnp.where(col == o + j, entries * scale, u)
        uppers.append(jnp.where(col >= o + row, u, 0.0))
        inverses.append(jnp.where(col <= o + row, w, 0.0))
    return jnp.concatenate(uppers, axis=0), jnp.concatenate(inverses, axis=0)


def factor_half(where_ref, s_ref, u_ref, w_ref):
    one = jnp.full((8, B), 1.0, F32) * jnp.where(where_ref[0] >= 0, 1.0, 0.0)
    count = HALF // B
    at = lambda i: slice(i * B, (i + 1) * B)
    for k in range(count):
        here = at(k)
        upper, inverse = factor_block([s_ref[k * B + 8 * i : k * B + 8 * i + 8, here] for i in range(16)], one)
        u_ref[here, here] = upper
        w_ref[here, here] = inverse
        if k:
            u_ref[here, : k * B] = jnp.zeros((B, k * B), F32)
            w_ref[here, : k * B] = exact(inverse, s_ref[here, : k * B], ((1,), (0,)))
        if k + 1 == count:
            break
        e = (k + 1) * B
        w_ref[here, e:] = jnp.zeros((B, HALF - e), F32)
        follow = exact(inverse, s_ref[here, at(k + 1)], ((1,), (0,)))
        u_ref[here, at(k + 1)] = follow
        s_ref[at(k + 1), at(k + 1)] = s_ref[at(k + 1), at(k + 1)] - exact(follow, follow, ((0,), (0,)))
        if e + B < HALF:
            u_ref[here, e + B :] = exact(inverse, s_ref[here, e + B :], ((1,), (0,)))
        for i in range(k + 1, count):
            mult = u_ref[here, at(i)]
            begin = max(i, k + 2) * B
            if begin < HALF:
                s_ref[at(i), begin:] = s_ref[at(i), begin:] - exact(mult, u_ref[here, begin:], ((0,), (0,)))
            if k:
                s_ref[at(i), : k * B] = s_ref[at(i), : k * B] - exact(mult, w_ref[here, : k * B], ((0,), (0,)))
            s_ref[at(i), here] = -exact(mult, inverse, ((0,), (0,)))


def call(kernel, name, outs, scratch, *args):
    shapes = tuple(jax.ShapeDtypeStruct(shape, dtype) for shape, dtype in outs)
    return pl.pallas_call(
        kernel,
        out_shape=shapes,
        in_specs=[SMEM] + [VMEM] * (len(args) - 1),
        out_specs=tuple(VMEM for _ in outs),
        scratch_shapes=[pltpu.VMEM(shape, dtype) for shape, dtype in scratch],
        compiler_params=pltpu.CompilerParams(vmem_limit_bytes=LIMIT),
        name=name,
    )(*args)


def prepare_kernel(where_ref, top_ref, g1_ref, g2_ref, g3_ref, mine_ref, tail_ref):
    z4 = where_ref[1] & 3
    for s, ref in enumerate((None, g1_ref, g2_ref, g3_ref)):
        piece = top_ref[pl.ds(0, 64, stride=12), :] if ref is None else ref[...]
        mine_ref[pl.ds(z4 ^ s, 1)] = piece[None]
    tail_ref[...] = top_ref[384:, :]


def share_kernel(where_ref, top_ref, moved_ref, share_ref):
    for d in range(12):
        share_ref[d] = jnp.where(
            where_ref[0] >= 2, moved_ref[pl.ds(d, 32, stride=12), :], top_ref[pl.ds(d, 32, stride=12), :]
        )


def choose_kernel(where_ref, own_ref, plus_ref, minus_ref, two_ref, a_ref, b_ref):
    orders = (
        (own_ref, minus_ref),
        (plus_ref, own_ref),
        (two_ref, plus_ref),
        (minus_ref, two_ref),
    )
    for x, (first, second) in enumerate(orders):

        @pl.when(where_ref[0] == x)
        def _():
            a_ref[...] = first[...]
            b_ref[...] = second[...]


def pack_kernel(where_ref, a_ref, g1_ref, g2_ref, g3_ref, b_ref, bo_ref, a2_ref, b2_ref):
    y = where_ref[2]
    core = where_ref[3]
    for s, ref in enumerate((a_ref, g1_ref, g2_ref, g3_ref)):
        for target in range(2):

            @pl.when(((y - target) & 3) == s)
            def _():
                a2_ref[target] = ref[...]

    b2_ref[pl.ds(core, 1)] = b_ref[...][None]
    b2_ref[pl.ds(1 - core, 1)] = bo_ref[...][None]


def first_kernel(where_ref, own_ref, other_ref, rows_ref, rows_other_ref, u_ref, w_ref, pair_ref, s_ref):
    core = where_ref[3]
    for y in range(2):
        s_ref[:, pl.ds(pl.multiple_of(y * 256 + core * B, B), B)] = own_ref[y]
        s_ref[:, pl.ds(pl.multiple_of(y * 256 + (1 - core) * B, B), B)] = other_ref[y]
    pair_ref[pl.ds(core, 1)] = rows_ref[...][None]
    pair_ref[pl.ds(1 - core, 1)] = rows_other_ref[...][None]
    factor_half(where_ref, s_ref, u_ref, w_ref)


def second_kernel(
    where_ref, g0_ref, g1_ref, g2_ref, g3_ref, ua_ref, wa_ref, w_ref, piece_ref, raw_ref, s_ref, u_ref
):
    for s, ref in enumerate((g0_ref, g1_ref, g2_ref, g3_ref)):
        for core in range(2):
            lanes = pl.ds(pl.multiple_of(((where_ref[2] - s) & 3) * 256 + core * B, B), B)
            raw_ref[:, lanes] = ref[core]
    cross = exact(wa_ref[...], raw_ref[:, :HALF], ((1,), (1,)))
    u_ref[:HALF, HALF:] = cross
    s_ref[...] = raw_ref[:, HALF:] - exact(cross, cross, ((0,), (0,)))
    part = dot3(split(cross), split(wa_ref[...]), ((0,), (0,)))
    w_ref[:HALF, :HALF] = wa_ref[...]
    w_ref[:HALF, HALF:] = jnp.zeros((HALF, HALF), F32)
    u_ref[:HALF, :HALF] = ua_ref[...]
    u_ref[HALF:, :HALF] = jnp.zeros((HALF, HALF), F32)
    lower = w_ref.at[HALF:, HALF:]
    factor_half(where_ref, s_ref, u_ref.at[HALF:, HALF:], lower)
    w_ref[HALF:, :HALF] = -dot3(split(lower[...]), split(part), ((1,), (0,)))
    row_rank = where_ref[0] * 8 + where_ref[1]
    mine = pl.ds(pl.multiple_of((where_ref[2] * 2 + where_ref[3]) * B, B), B)
    block = u_ref[mine, pl.ds(pl.multiple_of(((row_rank & 15) // 2) * B, B), B)].T
    piece_ref[...] = jnp.where(row_rank % 2 == 0, block[:64], block[64:])


def rows_kernel(
    where_ref, g0_ref, g1_ref, g2_ref, g3_ref, piece_ref, w_ref,
    high_ref, low_ref, slab_ref, ah_ref, al_ref, wh_ref, wl_ref, x_ref,
):
    y = where_ref[2]
    core = where_ref[3]
    for s, ref in enumerate((g0_ref, g1_ref, g2_ref, g3_ref)):
        for at in range(2):
            lanes = pl.ds(pl.multiple_of(((y - s) & 3) * 256 + at * B, B), B)
            ah_ref[:, lanes], al_ref[:, lanes] = split(ref[at])
    step = 256
    for k in range(0, FULL, step):
        wh_ref[k : k + step, :], wl_ref[k : k + step, :] = split(w_ref[k : k + step, :])
    for k in range(0, FULL, step):
        e = k + step
        x_ref[:, k:e] = dot3((ah_ref[:, :e], al_ref[:, :e]), (wh_ref[k:e, :e], wl_ref[k:e, :e]), ((1,), (1,)))
    row_rank = where_ref[0] * 8 + where_ref[1]
    mine = pl.ds(pl.multiple_of((y * 2 + core) * B, B), B)
    slab_ref[...] = x_ref[:, mine]
    for k in range(0, FULL, step):
        e = k + step
        ah_ref[:, k:e], al_ref[:, k:e] = split(x_ref[:, k:e])
    for j in range(0, FULL, step):
        e = j + step
        value = dot3((ah_ref[:, j:], al_ref[:, j:]), (wh_ref[j:, j:e], wl_ref[j:, j:e]), ((1,), (0,)))
        high_ref[:, j:e], low_ref[:, j:e] = split(value)

    @pl.when(row_rank < 16)
    def _():
        slab_ref[:64, :] = piece_ref[...]


def trailing_kernel(where_ref, a_ref, bulk_ref, high_ref, low_ref, slab_ref, out_ref, bh_ref, bl_ref):
    rows = high_ref.shape[0]
    row_rank = where_ref[0] * 8 + where_ref[1]
    gone = (row_rank < 16) & (lax.broadcasted_iota(jnp.int32, (rows, B), 0) < 64)
    pair = pl.program_id(0)
    for p in range(2):
        for z in range(8):
            for part in range(2):
                source = (8 * p if part == 0 else 24 - 8 * p) + z
                r = HALF * p + 64 * z + 32 * part
                for t in range(2):
                    high, low = split(bulk_ref[source, t])
                    bh_ref[r : r + 32, t * B : (t + 1) * B] = high
                    bl_ref[r : r + 32, t * B : (t + 1) * B] = low
    made = dot3((high_ref[...], low_ref[...]), (bh_ref[...], bl_ref[...]), ((1,), (0,)))
    for t in range(2):
        at = pl.ds(2 * pair + t, rows, stride=12)
        value = a_ref[at, :] - made[:, t * B : (t + 1) * B]
        out_ref[at, :] = jnp.where(gone, 0.0, value)

    @pl.when(pair == 0)
    def _():
        out_ref[pl.ds(0, rows, stride=12), :] = slab_ref[...]


def trailing(where, a, bulk, high, low, slab):
    whole = lambda v: pl.BlockSpec(v.shape, lambda i: (0,) * v.ndim)
    return pl.pallas_call(
        trailing_kernel,
        out_shape=jax.ShapeDtypeStruct(a.shape, F32),
        grid=(6,),
        in_specs=[
            SMEM,
            whole(a),
            pl.BlockSpec((32, 2, 32, B), lambda i: (0, i, 0, 0)),
            whole(high),
            whole(low),
            whole(slab),
        ],
        out_specs=whole(a),
        scratch_shapes=[pltpu.VMEM((FULL, 2 * B), BF16), pltpu.VMEM((FULL, 2 * B), BF16)],
        compiler_params=pltpu.CompilerParams(vmem_limit_bytes=LIMIT),
        name="trailing",
    )(where, a, bulk, high, low, slab)


def row_pairs(f):
    return [(x * 8 + z, (f(x, z)[0] % 4) * 8 + f(x, z)[1] % 8) for x in range(4) for z in range(8)]


def col_shift(s):
    return [(c, (c + 2 * s) % 8) for c in range(8)]


def swap_core(value):
    return lax.ppermute(value, "col", [(c, c ^ 1) for c in range(8)])


def from_x(source, target):
    return [(source * 8 + z, target * 8 + z) for z in range(8)]


def shards(front):
    lin = front.reshape(-1, B)
    rows = 384
    r = lax.axis_index("row")
    c = lax.axis_index("col")
    x, z, y, core = r // 8, r % 8, c // 2, c % 2
    where = jnp.stack([x, z, y, core]).astype(jnp.int32)

    top = lin[:768]
    piece = lax.slice(lin, (0, 0), (768, B), (12, 1))
    near = [lax.ppermute(piece, "row", row_pairs(lambda x, z: (x, z ^ s))) for s in (1, 2, 3)]
    mine, tail = call(
        prepare_kernel, "prepare", [((4, 64, B), F32), ((384, B), F32)], [], where, top, *near
    )
    across = lax.ppermute(mine, "row", row_pairs(lambda x, z: (x, z + 4)))
    moved = lax.ppermute(tail, "row", from_x(0, 3) + from_x(1, 2))
    (share,) = call(share_kernel, "share", [((12, 32, B), F32)], [], where, top, moved)
    bulk = lax.all_gather(share, "row", axis=0)

    both = jnp.where(z < 4, jnp.stack([mine, across]), jnp.stack([across, mine])).reshape(HALF, B)
    got = [lax.ppermute(both, "row", row_pairs(lambda x, z: (x + s, z))) for s in (1, 3, 2)]
    block = ((HALF, B), F32)
    a, b = call(choose_kernel, "choose", [block, block], [], where, both, *got)
    near = [
        lax.ppermute(a, "col", [(c, (c + 2 * s) % 8) for c in range(4)]) for s in (1, 2, 3)
    ]
    pair = ((2, HALF, B), F32)
    a2, b2 = call(pack_kernel, "pack", [pair, pair], [], where, a, *near, b, swap_core(b))
    near_b = [lax.ppermute(b2, "col", col_shift(s)) for s in (1, 2, 3)]
    slab = lax.slice(lin, (0, 0), lin.shape, (12, 1))
    square = ((HALF, HALF), F32)
    ua, wa, s2 = call(
        first_kernel, "first", [square, square, ((2, rows, B), F32)], [square],
        where, a2, swap_core(a2), slab, swap_core(slab),
    )
    near_s = [lax.ppermute(s2, "col", col_shift(s)) for s in (1, 2, 3)]
    whole = (FULL, FULL)
    w, piece = call(
        second_kernel, "second", [(whole, F32), ((64, B), F32)], [((HALF, FULL), F32), square, (whole, F32)],
        where, b2, *near_b, ua, wa,
    )
    high, low, own_slab = call(
        rows_kernel, "rows", [((rows, FULL), BF16), ((rows, FULL), BF16), ((rows, B), F32)],
        [((rows, FULL), BF16)] * 2 + [((FULL, FULL), BF16)] * 2 + [((rows, FULL), F32)],
        where, s2, *near_s, piece, w,
    )
    out = trailing(where, lin, bulk, high, low, own_slab)
    return out.reshape(front.shape)


def solution(mesh):
    spec = P(None, "row", None, None, "col", None)
    return jax.shard_map(shards, mesh=mesh, in_specs=(spec,), out_specs=spec, check_vma=False)
```

```python
import functools

import jax
import jax.numpy as jnp
from jax import lax
from jax.experimental import pallas as pl
from jax.experimental.pallas import tpu as pltpu
from jax.sharding import PartitionSpec as P

B = 128
HALF = 512
FULL = 1024
F32 = jnp.float32
BF16 = jnp.bfloat16
VMEM = pl.BlockSpec(memory_space=pltpu.VMEM)
SMEM = pl.BlockSpec(memory_space=pltpu.SMEM)
LIMIT = 30 * 1024 * 1024


def lane(tile, c):
    return jnp.broadcast_to(tile[:, c : c + 1], (8, B))


def sub(tile, i):
    return jnp.broadcast_to(tile[i : i + 1, :], (8, B))


def exact(left, right, dims):
    return lax.dot_general(
        left, right, (dims, ((), ())), precision=lax.Precision.HIGHEST, preferred_element_type=F32
    )


def split(value):
    high = value.astype(BF16)
    return high, (value - high.astype(F32)).astype(BF16)


def dot3(left, right, dims):
    mul = lambda a, b: lax.dot_general(a, b, (dims, ((), ())), preferred_element_type=F32)
    return mul(left[0], right[0]) + (mul(left[0], right[1]) + mul(left[1], right[0]))


def factor_block(rows, one):
    rows = list(rows)
    col = lax.broadcasted_iota(jnp.int32, (8, B), 1)
    row = lax.broadcasted_iota(jnp.int32, (8, B), 0)
    uppers, inverses = [], []
    for p in range(16):
        top = rows[p]
        o = 8 * p
        inside = (col >= o) & (col < o + 8)
        cols = [lane(top, o + j) * one for j in range(8)]
        a = {(i, j): sub(cols[j], i) for j in range(8) for i in range(j, 8)}
        unit = jnp.where(inside, (col - o == row).astype(F32), top)
        z = [sub(unit, j) for j in range(8)]
        more = p + 1 < 16
        if more:
            c = [lane(rows[p + 1], o + j) for j in range(8)]
            below = jnp.where(inside, 0.0, rows[p + 1])
        m, inv = {}, []
        for j in range(8):
            rcp = 1.0 / a[j, j]
            inv.append(rcp)
            for i in range(j + 1, 8):
                m[i, j] = a[i, j] * rcp
            if more:
                below = below - (c[j] * rcp) * z[j]
            for i in range(j + 1, 8):
                for k in range(j + 1, i + 1):
                    a[i, k] = a[i, k] - m[i, j] * a[k, j]
            for i in range(j + 1, 8):
                z[i] = z[i] - m[i, j] * z[j]
                if more:
                    c[i] = c[i] - m[i, j] * c[j]
        if more:
            rows[p + 1] = below
        if p + 2 < 16:
            v = [None] * 8
            for j in range(7, -1, -1):
                acc = z[j] * inv[j]
                for i in range(7, j, -1):
                    acc = acc - m[i, j] * v[i]
                v[j] = acc
            for q in range(p + 2, 16):
                t = [lane(rows[q], o + j) * v[j] for j in range(8)]
                s = ((t[0] + t[1]) + (t[2] + t[3])) + ((t[4] + t[5]) + (t[6] + t[7]))
                rows[q] = jnp.where(inside, 0.0, rows[q]) - s
        roots = [lax.rsqrt(a[j, j]) for j in range(8)]
        w = z[0] * roots[0]
        for i in range(1, 8):
            w = jnp.where(row == i, z[i] * roots[i], w)
        scale = a[0, 0] * roots[0]
        for i in range(1, 8):
            scale = jnp.where(row == i, a[i, i] * roots[i], scale)
        u = w
        for j in range(8):
            entries = jnp.ones((8, B), F32)
            for i in range(j):
                entries = jnp.where(row == i, m[j, i], entries)
            u = jnp.where(col == o + j, entries * scale, u)
        uppers.append(jnp.where(col >= o + row, u, 0.0))
        inverses.append(jnp.where(col <= o + row, w, 0.0))
    return jnp.concatenate(uppers, axis=0), jnp.concatenate(inverses, axis=0)


def factor_half(where_ref, s_ref, u_ref, w_ref):
    one = jnp.full((8, B), 1.0, F32) * jnp.where(where_ref[0] >= 0, 1.0, 0.0)
    count = HALF // B
    at = lambda i: slice(i * B, (i + 1) * B)
    for k in range(count):
        here = at(k)
        upper, inverse = factor_block([s_ref[k * B + 8 * i : k * B + 8 * i + 8, here] for i in range(16)], one)
        u_ref[here, here] = upper
        w_ref[here, here] = inverse
        if k:
            u_ref[here, : k * B] = jnp.zeros((B, k * B), F32)
            w_ref[here, : k * B] = exact(inverse, s_ref[here, : k * B], ((1,), (0,)))
        if k + 1 == count:
            break
        e = (k + 1) * B
        w_ref[here, e:] = jnp.zeros((B, HALF - e), F32)
        follow = exact(inverse, s_ref[here, at(k + 1)], ((1,), (0,)))
        u_ref[here, at(k + 1)] = follow
        s_ref[at(k + 1), at(k + 1)] = s_ref[at(k + 1), at(k + 1)] - exact(follow, follow, ((0,), (0,)))
        if e + B < HALF:
            u_ref[here, e + B :] = exact(inverse, s_ref[here, e + B :], ((1,), (0,)))
        for i in range(k + 1, count):
            mult = u_ref[here, at(i)]
            begin = max(i, k + 2) * B
            if begin < HALF:
                s_ref[at(i), begin:] = s_ref[at(i), begin:] - exact(mult, u_ref[here, begin:], ((0,), (0,)))
            if k:
                s_ref[at(i), : k * B] = s_ref[at(i), : k * B] - exact(mult, w_ref[here, : k * B], ((0,), (0,)))
            s_ref[at(i), here] = -exact(mult, inverse, ((0,), (0,)))


def call(kernel, name, outs, scratch, *args):
    shapes = tuple(jax.ShapeDtypeStruct(shape, dtype) for shape, dtype in outs)
    return pl.pallas_call(
        kernel,
        out_shape=shapes,
        in_specs=[SMEM] + [VMEM] * (len(args) - 1),
        out_specs=tuple(VMEM for _ in outs),
        scratch_shapes=[pltpu.VMEM(shape, dtype) for shape, dtype in scratch],
        compiler_params=pltpu.CompilerParams(vmem_limit_bytes=LIMIT),
        name=name,
    )(*args)


def prepare_kernel(where_ref, top_ref, moved_ref, g1_ref, g2_ref, g3_ref, mine_ref, share_ref):
    z4 = where_ref[1] & 3
    for s, ref in enumerate((None, g1_ref, g2_ref, g3_ref)):
        piece = top_ref[pl.ds(0, 64, stride=12), :] if ref is None else ref[...]
        mine_ref[pl.ds(z4 ^ s, 1)] = piece[None]
    for d in range(12):
        share_ref[d] = jnp.where(
            where_ref[0] >= 2, moved_ref[pl.ds(d, 32, stride=12), :], top_ref[pl.ds(d, 32, stride=12), :]
        )


def choose_kernel(where_ref, own_ref, plus_ref, minus_ref, two_ref, a_ref, b_ref):
    orders = (
        (own_ref, minus_ref),
        (plus_ref, own_ref),
        (two_ref, plus_ref),
        (minus_ref, two_ref),
    )
    for x, (first, second) in enumerate(orders):

        @pl.when(where_ref[0] == x)
        def _():
            a_ref[...] = first[...]
            b_ref[...] = second[...]


def pack_kernel(where_ref, a_ref, g1_ref, g2_ref, g3_ref, b_ref, bo_ref, a2_ref, b2_ref):
    y = where_ref[2]
    core = where_ref[3]
    for s, ref in enumerate((a_ref, g1_ref, g2_ref, g3_ref)):
        for target in range(2):

            @pl.when(((y - target) & 3) == s)
            def _():
                a2_ref[target] = ref[...]

    b2_ref[pl.ds(core, 1)] = b_ref[...][None]
    b2_ref[pl.ds(1 - core, 1)] = bo_ref[...][None]


def first_kernel(where_ref, own_ref, other_ref, rows_ref, rows_other_ref, u_ref, w_ref, pair_ref, s_ref):
    core = where_ref[3]
    for y in range(2):
        s_ref[:, pl.ds(pl.multiple_of(y * 256 + core * B, B), B)] = own_ref[y]
        s_ref[:, pl.ds(pl.multiple_of(y * 256 + (1 - core) * B, B), B)] = other_ref[y]
    pair_ref[pl.ds(core, 1)] = rows_ref[...][None]
    pair_ref[pl.ds(1 - core, 1)] = rows_other_ref[...][None]
    factor_half(where_ref, s_ref, u_ref, w_ref)


def second_kernel(
    where_ref, g0_ref, g1_ref, g2_ref, g3_ref, ua_ref, wa_ref, w_ref, piece_ref, raw_ref, s_ref, u_ref
):
    for s, ref in enumerate((g0_ref, g1_ref, g2_ref, g3_ref)):
        for core in range(2):
            lanes = pl.ds(pl.multiple_of(((where_ref[2] - s) & 3) * 256 + core * B, B), B)
            raw_ref[:, lanes] = ref[core]
    cross = exact(wa_ref[...], raw_ref[:, :HALF], ((1,), (1,)))
    u_ref[:HALF, HALF:] = cross
    s_ref[...] = raw_ref[:, HALF:] - exact(cross, cross, ((0,), (0,)))
    part = dot3(split(cross), split(wa_ref[...]), ((0,), (0,)))
    w_ref[:HALF, :HALF] = wa_ref[...]
    w_ref[:HALF, HALF:] = jnp.zeros((HALF, HALF), F32)
    u_ref[:HALF, :HALF] = ua_ref[...]
    u_ref[HALF:, :HALF] = jnp.zeros((HALF, HALF), F32)
    lower = w_ref.at[HALF:, HALF:]
    factor_half(where_ref, s_ref, u_ref.at[HALF:, HALF:], lower)
    w_ref[HALF:, :HALF] = -dot3(split(lower[...]), split(part), ((1,), (0,)))
    row_rank = where_ref[0] * 8 + where_ref[1]
    mine = pl.ds(pl.multiple_of((where_ref[2] * 2 + where_ref[3]) * B, B), B)
    block = u_ref[mine, pl.ds(pl.multiple_of(((row_rank & 15) // 2) * B, B), B)].T
    piece_ref[...] = jnp.where(row_rank % 2 == 0, block[:64], block[64:])


def rows_kernel(
    where_ref, g0_ref, g1_ref, g2_ref, g3_ref, piece_ref, w_ref,
    high_ref, low_ref, slab_ref, ah_ref, al_ref, wh_ref, wl_ref, x_ref,
):
    y = where_ref[2]
    core = where_ref[3]
    for s, ref in enumerate((g0_ref, g1_ref, g2_ref, g3_ref)):
        for at in range(2):
            lanes = pl.ds(pl.multiple_of(((y - s) & 3) * 256 + at * B, B), B)
            ah_ref[:, lanes], al_ref[:, lanes] = split(ref[at])
    step = 256
    for k in range(0, FULL, step):
        wh_ref[k : k + step, :], wl_ref[k : k + step, :] = split(w_ref[k : k + step, :])
    for k in range(0, FULL, step):
        e = k + step
        x_ref[:, k:e] = dot3((ah_ref[:, :e], al_ref[:, :e]), (wh_ref[k:e, :e], wl_ref[k:e, :e]), ((1,), (1,)))
    row_rank = where_ref[0] * 8 + where_ref[1]
    mine = pl.ds(pl.multiple_of((y * 2 + core) * B, B), B)
    slab_ref[...] = x_ref[:, mine]
    for k in range(0, FULL, step):
        e = k + step
        ah_ref[:, k:e], al_ref[:, k:e] = split(x_ref[:, k:e])
    for j in range(0, FULL, step):
        e = j + step
        value = dot3((ah_ref[:, j:], al_ref[:, j:]), (wh_ref[j:, j:e], wl_ref[j:, j:e]), ((1,), (0,)))
        high_ref[:, j:e], low_ref[:, j:e] = split(value)

    @pl.when(row_rank < 16)
    def _():
        slab_ref[:64, :] = piece_ref[...]


def trailing_kernel(where_ref, a_ref, bulk_ref, high_ref, low_ref, slab_ref, out_ref, bh_ref, bl_ref):
    rows = high_ref.shape[0]
    row_rank = where_ref[0] * 8 + where_ref[1]
    gone = (row_rank < 16) & (lax.broadcasted_iota(jnp.int32, (rows, B), 0) < 64)
    pair = pl.program_id(0)
    for p in range(2):
        for z in range(8):
            for part in range(2):
                source = (8 * p if part == 0 else 24 - 8 * p) + z
                r = HALF * p + 64 * z + 32 * part
                for t in range(2):
                    high, low = split(bulk_ref[source, t])
                    bh_ref[r : r + 32, t * B : (t + 1) * B] = high
                    bl_ref[r : r + 32, t * B : (t + 1) * B] = low
    made = dot3((high_ref[...], low_ref[...]), (bh_ref[...], bl_ref[...]), ((1,), (0,)))
    for t in range(2):
        at = pl.ds(2 * pair + t, rows, stride=12)
        value = a_ref[at, :] - made[:, t * B : (t + 1) * B]
        out_ref[at, :] = jnp.where(gone, 0.0, value)

    @pl.when(pair == 0)
    def _():
        out_ref[pl.ds(0, rows, stride=12), :] = slab_ref[...]


def trailing(where, a, bulk, high, low, slab):
    whole = lambda v: pl.BlockSpec(v.shape, lambda i: (0,) * v.ndim)
    return pl.pallas_call(
        trailing_kernel,
        out_shape=jax.ShapeDtypeStruct(a.shape, F32),
        grid=(6,),
        in_specs=[
            SMEM,
            whole(a),
            pl.BlockSpec((32, 2, 32, B), lambda i: (0, i, 0, 0)),
            whole(high),
            whole(low),
            whole(slab),
        ],
        out_specs=whole(a),
        scratch_shapes=[pltpu.VMEM((FULL, 2 * B), BF16), pltpu.VMEM((FULL, 2 * B), BF16)],
        compiler_params=pltpu.CompilerParams(vmem_limit_bytes=LIMIT),
        name="trailing",
    )(where, a, bulk, high, low, slab)


def row_pairs(f):
    return [(x * 8 + z, (f(x, z)[0] % 4) * 8 + f(x, z)[1] % 8) for x in range(4) for z in range(8)]


def col_shift(s):
    return [(c, (c + 2 * s) % 8) for c in range(8)]


def swap_core(value):
    return lax.ppermute(value, "col", [(c, c ^ 1) for c in range(8)])


def from_x(source, target):
    return [(source * 8 + z, target * 8 + z) for z in range(8)]


def shards(front):
    lin = front.reshape(-1, B)
    rows = 384
    r = lax.axis_index("row")
    c = lax.axis_index("col")
    x, z, y, core = r // 8, r % 8, c // 2, c % 2
    where = jnp.stack([x, z, y, core]).astype(jnp.int32)

    top = lin[:768]
    piece = lax.slice(lin, (0, 0), (768, B), (12, 1))
    near = [lax.ppermute(piece, "row", row_pairs(lambda x, z: (x, z ^ s))) for s in (1, 2, 3)]
    moved = lax.ppermute(top[384:], "row", from_x(0, 3) + from_x(1, 2))
    mine, share = call(
        prepare_kernel, "prepare", [((4, 64, B), F32), ((12, 32, B), F32)], [], where, top, moved, *near
    )
    across = lax.ppermute(mine, "row", row_pairs(lambda x, z: (x, z + 4)))
    bulk = lax.all_gather(share, "row", axis=0)

    both = jnp.where(z < 4, jnp.stack([mine, across]), jnp.stack([across, mine])).reshape(HALF, B)
    got = [lax.ppermute(both, "row", row_pairs(lambda x, z: (x + s, z))) for s in (1, 3, 2)]
    block = ((HALF, B), F32)
    a, b = call(choose_kernel, "choose", [block, block], [], where, both, *got)
    near = [
        lax.ppermute(a, "col", [(c, (c + 2 * s) % 8) for c in range(4)]) for s in (1, 2, 3)
    ]
    pair = ((2, HALF, B), F32)
    a2, b2 = call(pack_kernel, "pack", [pair, pair], [], where, a, *near, b, swap_core(b))
    near_b = [lax.ppermute(b2, "col", col_shift(s)) for s in (1, 2, 3)]
    slab = lax.slice(lin, (0, 0), lin.shape, (12, 1))
    square = ((HALF, HALF), F32)
    ua, wa, s2 = call(
        first_kernel, "first", [square, square, ((2, rows, B), F32)], [square],
        where, a2, swap_core(a2), slab, swap_core(slab),
    )
    near_s = [lax.ppermute(s2, "col", col_shift(s)) for s in (1, 2, 3)]
    whole = (FULL, FULL)
    w, piece = call(
        second_kernel, "second", [(whole, F32), ((64, B), F32)], [((HALF, FULL), F32), square, (whole, F32)],
        where, b2, *near_b, ua, wa,
    )
    high, low, own_slab = call(
        rows_kernel, "rows", [((rows, FULL), BF16), ((rows, FULL), BF16), ((rows, B), F32)],
        [((rows, FULL), BF16)] * 2 + [((FULL, FULL), BF16)] * 2 + [((rows, FULL), F32)],
        where, s2, *near_s, piece, w,
    )
    out = trailing(where, lin, bulk, high, low, own_slab)
    return out.reshape(front.shape)


def solution(mesh):
    spec = P(None, "row", None, None, "col", None)
    return jax.shard_map(shards, mesh=mesh, in_specs=(spec,), out_specs=spec, check_vma=False)
```
